32 devices in a mesh: groups: 2 (over x), pool: 16 (over z, y, core).
Axes of the slice: x: 2, y: 2, z: 4, core: 2. Of those that a mesh axis runs over, the one named last changes fastest.
Arguments:
- tokens: bfloat16 [64, 8192], P(('groups', 'pool')), parts along dimension 0, may hold values from -6 to 6
- base_projection_weight: bfloat16 [8192, 8192], P(None, 'pool'), may hold values from -0.0625 to 0.0625
- adapter_down_weight: bfloat16 [2048, 8192], P('pool'), may hold values from -0.0625 to 0.0625
- adapter_up_weight: bfloat16 [2048, 8192], P('pool'), may hold values from -0.5 to 0.5
- request_adapter: int32 [64, 1], P('groups'), parts along dimension 0, may hold values from 0 to 15; in each aligned block of 32 rows (0 to 31, 32 to 63, ...) at most 3 rows name the same one
- adapter_block_count: int32 [16], replicated, may hold values from 1 to 8, as said below
- adapter_store_slot: int32 [16], replicated, may hold values from 0 to 15, each once
Outputs:
- projected: bfloat16 [64, 8192], P(('groups', 'pool')), parts along dimension 0
The draws below stay inside these ranges and needn't reach their ends.
There are 2 independent parts, one for each index of `groups`. The reference program is written for one: setup_inputs(seed, part) draws one part's arguments, and reference() takes and returns one part's arrays. A program takes and returns all parts, laid end to end along the dimension named above; an argument that names none is the same for every part. Nothing has to cross between parts.
Inputs may be any that keep to these rules, and one draw needn't show every extreme that they name: `adapter_block_count`: each adapter has 1 to 8 blocks; some adapter has exactly 8. `request_adapter`: among all requests of the part no adapter is named more than 3 times; some adapter is named exactly 3 times.
All inputs are finite; a program needn't handle non-finite values.
Results may differ from the reference program's by a relative error of at most 0.0046.
Values may be sent and summed in bfloat16 or wider, within the bound.
No kernel may reach another device: no remote copies, remote signals or barrier semaphores. Data moves between devices by JAX's collectives and lax.ppermute only.
A program may use at most 64 MiB of HBM per device.

```python
import math
import jax
import jax.numpy as jnp
import numpy as np
from jax import lax

MODEL_WIDTH = 8192
ADAPT_DEV = 1
RANK_BLOCK = 16
MAXIMUM_BLOCKS = 8
MOSTB = 3
BLK_DEV = 8
REQS = 32
NADAPT = 16
STORE_RANK_ROWS = 2048


def draw_adapter_block_count(key, part):
    key = jax.random.fold_in(key, 5)
    ranks = jax.random.randint(key, (NADAPT,), 1, MAXIMUM_BLOCKS + 1).astype(jnp.int32)
    return ranks.at[0].set(MAXIMUM_BLOCKS)


def shard_levels(key, dims, pieces, low, high):
    factor_of, own = 1.0, jax.random.fold_in(key, 6)
    for position, shards_of in pieces:
        heights = jnp.exp(jax.random.uniform(jax.random.fold_in(own, position), (shards_of,), jnp.float32, low / len(pieces), high / len(pieces)))
        factor_of = factor_of * jnp.repeat(heights, dims[position] // shards_of).reshape([-1 if axis == position else 1 for axis in range(len(dims))])
    return factor_of


def routed_block(rng, own, number, rows, amount, top, bound, slope):
    order = jax.random.permutation(rng, amount)
    packed, ordinary = load_shares(amount, rows * top, bound, slope, True), load_shares(amount, rows * top, bound, slope, False)
    places = jnp.arange(amount)

    def named(tallies, turn):
        used = int((tallies > 0).sum())
        fixed = max(1, used // 4)
        passed = fixed + (places - fixed + turn * (used - fixed)) % max(1, amount - fixed)
        return jnp.zeros((amount,), jnp.int32).at[order[jnp.where(places < fixed, places, passed)]].set(jnp.asarray(tallies, jnp.int32))

    tallies = jnp.where(number % 4 == 0, named(packed, number // 4), named(ordinary, number - number // 4 - 1))
    mixed = jax.random.permutation(jax.random.fold_in(own, 3), amount)
    source_of, receiver = mixed[0:amount // 2 * 2:2], mixed[1:amount // 2 * 2:2]
    room = jnp.minimum(tallies[source_of] - 1, bound - tallies[receiver]) // 2
    room = jnp.where((source_of == order[0]) | (receiver == order[0]) | (tallies[receiver] == 0), 0, jnp.maximum(room, 0))
    passed = jax.random.randint(jax.random.fold_in(own, 4), (amount // 2,), 0, 1 << 20) % (room + 1)
    tallies = tallies.at[source_of].add(-passed).at[receiver].add(passed)
    labels = jnp.searchsorted(jnp.cumsum(tallies), jnp.arange(rows * top), side="right").astype(jnp.int32)
    grid = labels.reshape(top, rows).T
    grid = grid[jax.random.permutation(jax.random.fold_in(own, 1), rows)]
    turn = jax.random.randint(jax.random.fold_in(own, 2), (rows, 1), 0, top)
    return jnp.take_along_axis(grid, (jnp.arange(top)[None, :] + turn) % top, axis=1)


def load_shares(count, total, bound, slope, full):
    weights = [(1 << 20) // math.isqrt(grade ** slope) + 1 for grade in range(1, count + 1)]
    largest = bound if full else min(bound, max(-(-total // count), total * weights[0] // sum(weights)))
    least = 1 if total - largest >= count - 1 else 0
    holding, rest = [largest] + [least] * (count - 1), total - largest - least * (count - 1)
    while rest > 0:
        movable = [i for i in range(1, count) if holding[i] < largest] or [i for i in range(1, count) if holding[i] < bound]
        mass, remaining = sum([weights[i] for i in movable]), rest
        for i in movable:
            extra = min(bound - holding[i], max(1, remaining * weights[i] // mass), rest)
            holding[i] = holding[i] + extra
            rest = rest - extra
    return np.array(holding)


def noise(stream_key, dims, scale, most, pieces=(), held_as=jnp.bfloat16):
    factor_of = shard_levels(stream_key, dims, pieces, -0.22, 0.18) if pieces else 1.0
    array = jax.random.normal(stream_key, dims, jnp.float32) * scale * factor_of
    return jnp.minimum(jnp.maximum(array, -most), most).astype(held_as)


def setup_inputs(seed: int = 0, part: int = 0) -> dict:
    seeds = jax.random.split(jax.random.key(seed), 8)
    part_keys = jax.random.split(jax.random.fold_in(seeds[7], part), 8)
    tokens = noise(part_keys[0], (REQS, MODEL_WIDTH), 1.0, 6.0, ((0, 16),))
    base_projection_weight = noise(seeds[1], (MODEL_WIDTH, MODEL_WIDTH), MODEL_WIDTH ** -0.5, 0.0625, ((1, 16),))
    adapter_down_weight = noise(seeds[2], (STORE_RANK_ROWS, MODEL_WIDTH), MODEL_WIDTH ** -0.5, 0.0625, ((0, 16),))
    adapter_up_weight = noise(seeds[3], (STORE_RANK_ROWS, MODEL_WIDTH), (RANK_BLOCK * MAXIMUM_BLOCKS) ** -0.5, 0.5, ((0, 16),))
    request_adapter_keys = jax.random.split(jax.random.fold_in(part_keys[4], 1), REQS // REQS)
    request_adapter_turns = jax.random.permutation(jax.random.fold_in(part_keys[4], 3), REQS // REQS)
    request_adapter = jax.vmap(lambda own, number: routed_block(jax.random.fold_in(part_keys[4], 2), own, number, REQS, NADAPT, 1, MOSTB, 2))(request_adapter_keys, request_adapter_turns).reshape((REQS, 1))
    adapter_block_count = draw_adapter_block_count(jax.random.fold_in(seeds[7], 71), part)
    adapter_store_slot = jax.random.permutation(seeds[6], NADAPT).astype(jnp.int32)
    return {"tokens": tokens, "base_projection_weight": base_projection_weight, "adapter_down_weight": adapter_down_weight, "adapter_up_weight": adapter_up_weight, "request_adapter": request_adapter, "adapter_block_count": adapter_block_count, "adapter_store_slot": adapter_store_slot}


def reference(tokens, base_projection_weight, adapter_down_weight, adapter_up_weight, request_adapter, adapter_block_count, adapter_store_slot):
    nadapt = adapter_block_count.shape[0]
    base = jnp.dot(tokens, base_projection_weight, preferred_element_type=jnp.float32)
    rank_by_slot = jnp.zeros((nadapt,), jnp.int32).at[adapter_store_slot].set(adapter_block_count)
    per_device = rank_by_slot.reshape(-1, ADAPT_DEV)
    start_in = (jnp.cumsum(per_device, axis=1).astype(jnp.int32) - per_device).reshape(-1)
    owner = adapter_store_slot // ADAPT_DEV
    first = ((owner * BLK_DEV + start_in[adapter_store_slot]) * RANK_BLOCK).astype(jnp.int32)
    limit = (adapter_block_count * RANK_BLOCK).astype(jnp.int32)
    rank_extent = MAXIMUM_BLOCKS * RANK_BLOCK
    padded_down_rows = jnp.concatenate([adapter_down_weight, jnp.zeros((rank_extent, adapter_down_weight.shape[1]), adapter_down_weight.dtype)], axis=0)
    padded_up_rows = jnp.concatenate([adapter_up_weight, jnp.zeros((rank_extent, adapter_up_weight.shape[1]), adapter_up_weight.dtype)], axis=0)

    def single(pair):
        row, adapter = pair
        begin = first[adapter].astype(jnp.int32)
        down_rows = lax.dynamic_slice_in_dim(padded_down_rows, begin, rank_extent, 0)
        up_rows = lax.dynamic_slice_in_dim(padded_up_rows, begin, rank_extent, 0)
        shrink = jnp.dot(down_rows, row, preferred_element_type=jnp.float32)
        keep = jnp.arange(rank_extent, dtype=jnp.int32) < limit[adapter]
        shrink = jnp.where(keep, shrink, jnp.float32(0.0)).astype(jnp.bfloat16)
        return jnp.dot(shrink, up_rows, preferred_element_type=jnp.float32).astype(jnp.bfloat16)

    delta = lax.map(single, (tokens, request_adapter[:, 0]))
    return (base + delta.astype(jnp.float32)).astype(jnp.bfloat16)
```

```python
import jax
import jax.numpy as jnp
from jax import lax
from jax.experimental import pallas as pl
from jax.experimental.pallas import tpu as pltpu
from jax.sharding import PartitionSpec as P

RANK_BLOCK = 16


def stages_of(devices):
    bits = [1 << k for k in range(1, devices.bit_length() - 1)]
    stages = [[b] for b in bits[:1]]
    rest = bits[1:]
    for k in range(0, len(rest), 2):
        low = rest[k]
        stages.append([low, rest[k + 1], low + rest[k + 1]] if k + 1 < len(rest) else [low])
    return stages


def exchange(array, mask, devices):
    return lax.ppermute(array, "pool", [(d, d ^ mask) for d in range(devices)])


def project_kernel(rows, where_ref, own_ref, keep_ref, near_ref, far_ref, base_ref, down_ref, up_ref, near_out, far_out):
    half = near_ref.shape[0]
    width = base_ref.shape[1]
    device = where_ref[0]
    x = jnp.concatenate([near_ref[...], far_ref[...]], axis=0)
    shrink = lax.dot_general(x, down_ref[...], (((1,), (1,)), ((), ())), preferred_element_type=jnp.float32)
    shrink = jnp.where(keep_ref[...] > 0, shrink, 0.0).astype(jnp.bfloat16)
    base = jnp.dot(x, base_ref[...], preferred_element_type=jnp.float32)
    to = lax.broadcasted_iota(jnp.int32, (half, half), 0)
    of = lax.broadcasted_iota(jnp.int32, (half, half), 1)
    order = to == (of ^ (rows * (device // 2)))
    narrow, wide = order.astype(jnp.bfloat16), order.astype(jnp.float32)
    lanes = max(width, 128)
    columns = pl.ds(pl.multiple_of(device * width // lanes * lanes, lanes), lanes)
    lane = lax.broadcasted_iota(jnp.int32, (half, lanes), 1)
    inside = lane // width == device % (lanes // width)
    for part, out in ((0, near_out), (1, far_out)):
        span = slice(part * half, (part + 1) * half)
        ranked = jnp.dot(narrow, shrink[span], preferred_element_type=jnp.float32)
        ranked = jnp.where(own_ref[span] > 0, ranked, 0.0).astype(jnp.bfloat16)
        placed = jnp.dot(wide, base[span], preferred_element_type=jnp.float32, precision=lax.Precision.HIGHEST)
        out[...] = jnp.dot(ranked, up_ref[...], preferred_element_type=jnp.float32).astype(jnp.bfloat16)
        placed = jnp.where(inside, jnp.concatenate([placed] * (lanes // width), axis=1), 0.0)
        out[:, columns] = (placed + out[:, columns].astype(jnp.float32)).astype(jnp.bfloat16)


def body(
    tokens,
    base_projection_weight,
    adapter_down_weight,
    adapter_up_weight,
    request_adapter,
    adapter_block_count,
    adapter_store_slot,
):
    device = lax.axis_index("pool")
    devices = lax.axis_size("pool")
    rows, model = tokens.shape
    half = devices // 2 * rows

    place = jnp.arange(2 * half, dtype=jnp.int32)
    core = (device % 2) ^ (place // half)
    request = ((place % half) // rows * 2 + core) * rows + place % rows
    mine = adapter_store_slot == device
    adapters = jnp.arange(mine.shape[0], dtype=jnp.int32)
    my_adapter = jnp.sum(jnp.where(mine, adapters, 0))
    my_rank = jnp.sum(jnp.where(mine, adapter_block_count, 0)) * RANK_BLOCK
    idents = request_adapter[:, 0]
    named = jnp.sum(jnp.where(request[:, None] == place[None, :], idents[None, :], 0), axis=1)
    own = (named == my_adapter).astype(jnp.int32)[:, None]
    keep = (jnp.arange(adapter_down_weight.shape[0], dtype=jnp.int32) < my_rank).astype(jnp.int32)[None, :]

    near = tokens
    for stage in stages_of(devices):
        near = jnp.concatenate([near] + [exchange(near, m, devices) for m in stage], axis=0)
    far = exchange(near, 1, devices)

    vmem = pl.BlockSpec(memory_space=pltpu.VMEM)
    near_out, far_out = pl.pallas_call(
        lambda *refs: project_kernel(rows, *refs),
        out_shape=[jax.ShapeDtypeStruct((half, model), jnp.bfloat16)] * 2,
        in_specs=[pl.BlockSpec(memory_space=pltpu.SMEM)] + [vmem] * 7,
        out_specs=[vmem] * 2,
        compiler_params=pltpu.CompilerParams(vmem_limit_bytes=40 * 1024 * 1024),
    )(
        device.astype(jnp.int32)[None],
        own,
        keep,
        near,
        far,
        pltpu.with_memory_space_constraint(base_projection_weight, pltpu.VMEM),
        pltpu.with_memory_space_constraint(adapter_down_weight, pltpu.VMEM),
        pltpu.with_memory_space_constraint(adapter_up_weight, pltpu.VMEM),
    )
    other = exchange(far_out, 1, devices)
    summed = (near_out.astype(jnp.float32) + other.astype(jnp.float32)).astype(jnp.bfloat16)
    summed = summed.reshape(devices // 2, rows, model)
    groups = [[d for d in range(devices) if d % 2 == c] for c in (0, 1)]
    pieces = lax.all_to_all(summed, "pool", 0, 0, tiled=True, axis_index_groups=groups)
    return jnp.sum(pieces.astype(jnp.float32), axis=0).astype(jnp.bfloat16)


def solution(mesh):
    return jax.shard_map(
        body,
        mesh=mesh,
        in_specs=(
            P(("groups", "pool"), None),
            P(None, "pool"),
            P("pool", None),
            P("pool", None),
            P("groups", None),
            P(),
            P(),
        ),
        out_specs=P(("groups", "pool"), None),
        check_vma=False,
    )
```

```python
import functools

import jax
import jax.numpy as jnp
from jax import lax
from jax.experimental import pallas as pl
from jax.experimental.pallas import tpu as pltpu
from jax.sharding import PartitionSpec as P

RANK_BLOCK = 16
LANES = 128
SPACE = pltpu.HBM


def stages_of(devices):
    bits = [1 << k for k in range(1, devices.bit_length() - 1)]
    stages = [[b] for b in bits[:1]]
    rest = bits[1:]
    for k in range(0, len(rest), 2):
        low = rest[k]
        stages.append([low, rest[k + 1], low + rest[k + 1]] if k + 1 < len(rest) else [low])
    return stages


def exchange(array, mask, devices):
    return lax.ppermute(array, "pool", [(d, d ^ mask) for d in range(devices)])


def canonical(rows, half, device):
    to = lax.broadcasted_iota(jnp.int32, (half, half), 0)
    of = lax.broadcasted_iota(jnp.int32, (half, half), 1)
    return to == (of ^ (rows * (device // 2)))


def mask_kernel(rows, extent, ident_ref, count_ref, slot_ref, out_ref):
    half = out_ref.shape[0]
    device = lax.axis_index("pool")

    def ranks(a, held):
        slot, count = slot_ref[a], count_ref[a] * RANK_BLOCK
        return jnp.where(slot == device, count, held[0]), jnp.where(slot == device ^ 1, count, held[1])

    rank, rank2 = lax.fori_loop(0, slot_ref.shape[0], ranks, (jnp.int32(0), jnp.int32(0)))
    row = lax.broadcasted_iota(jnp.int32, out_ref.shape, 0)
    col = lax.broadcasted_iota(jnp.int32, out_ref.shape, 1)

    def limits(q, held):
        request = (q // rows * 2 + device % 2) * rows + q % rows
        slot = slot_ref[ident_ref[request]]
        low = jnp.where(slot == device ^ 1, extent, 0)
        high = jnp.where(slot == device, rank, jnp.where(slot == device ^ 1, extent + rank2, 0))
        return jnp.where((row == q) & (col >= low) & (col < high), 1.0, held)

    out_ref[...] = lax.fori_loop(0, half, limits, jnp.zeros(out_ref.shape, jnp.float32), unroll=min(half, 16))


def delta_kernel(rows, mask_ref, near_ref, down_ref, down2_ref, up_ref, up2_ref, out_ref):
    half = near_ref.shape[0]
    extent = down_ref.shape[0]
    device = lax.axis_index("pool")
    mask = mask_ref[...]
    nt = (((1,), (1,)), ((), ()))
    order = canonical(rows, half, device).astype(jnp.bfloat16)
    ranked = []
    for ref, used in ((down_ref, mask[:, :extent]), (down2_ref, mask[:, extent:])):
        shrink = lax.dot_general(near_ref[...], ref[...], nt, preferred_element_type=jnp.float32)
        shrink = jnp.dot(order, shrink.astype(jnp.bfloat16), preferred_element_type=jnp.float32)
        ranked.append(jnp.where(used > 0, shrink, 0.0).astype(jnp.bfloat16))
    step = min(1024, out_ref.shape[1])
    for c in range(0, out_ref.shape[1], step):
        span = slice(c, c + step)
        out_ref[:, span] = (
            jnp.dot(ranked[0], up_ref[:, span], preferred_element_type=jnp.float32)
            + jnp.dot(ranked[1], up2_ref[:, span], preferred_element_type=jnp.float32)
        ).astype(jnp.bfloat16)


def base_kernel(near_ref, far_ref, weight_ref, near_out, far_out):
    half = near_ref.shape[0]
    x = jnp.concatenate([near_ref[...], far_ref[...]], axis=0)
    base = jnp.dot(x, weight_ref[...], preferred_element_type=jnp.float32)
    near_out[...] = base[:half]
    far_out[...] = base[half:]


def load_kernel(count, *refs):
    copies = [
        pltpu.make_async_copy(refs[i], refs[count + i], refs[2 * count].at[i]) for i in range(count)
    ]
    for copy in copies:
        copy.start()
    for copy in copies:
        copy.wait()


def load(*arrays):
    count = len(arrays)
    return pl.pallas_call(
        functools.partial(load_kernel, count),
        out_shape=[pltpu.VMEM(a.shape, a.dtype) for a in arrays],
        in_specs=[pl.BlockSpec(memory_space=SPACE)] * count,
        out_specs=[pl.BlockSpec(memory_space=pltpu.VMEM)] * count,
        scratch_shapes=[pltpu.SemaphoreType.DMA((count,))],
        cost_estimate=pl.CostEstimate(
            flops=0, bytes_accessed=sum(2 * a.size * a.dtype.itemsize for a in arrays), transcendentals=0
        ),
        compiler_params=pltpu.CompilerParams(vmem_limit_bytes=1024 * 1024),
        name="load",
    )(*[pltpu.with_memory_space_constraint(a, pltpu.HBM) for a in arrays])


def add_kernel(rows, delta_ref, base_ref, base2_ref, out_ref):
    half, width = base_ref.shape
    device = lax.axis_index("pool")
    order = canonical(rows, half, device).astype(jnp.float32)
    placed = [
        jnp.dot(order, ref[...], preferred_element_type=jnp.float32, precision=lax.Precision.HIGHEST)
        for ref in (base_ref, base2_ref)
    ]
    odd = device % 2 == 1
    both = jnp.concatenate(
        [jnp.where(odd, placed[1], placed[0]), jnp.where(odd, placed[0], placed[1])], axis=1
    )
    wide = 2 * width
    lanes = max(wide, LANES)
    columns = pl.ds(pl.multiple_of(device // 2 * wide // lanes * lanes, lanes), lanes)
    lane = lax.broadcasted_iota(jnp.int32, (half, lanes), 1)
    inside = lane // wide == device // 2 % (lanes // wide)
    both = jnp.where(inside, jnp.concatenate([both] * (lanes // wide), axis=1), 0.0)
    out_ref[...] = delta_ref[...]
    out_ref[:, columns] = (both + delta_ref[:, columns].astype(jnp.float32)).astype(jnp.bfloat16)


def body(
    tokens,
    base_projection_weight,
    adapter_down_weight,
    adapter_up_weight,
    request_adapter,
    adapter_block_count,
    adapter_store_slot,
):
    devices = lax.axis_size("pool")
    rows, model = tokens.shape
    half = devices // 2 * rows
    vmem, smem = pl.BlockSpec(memory_space=pltpu.VMEM), pl.BlockSpec(memory_space=pltpu.SMEM)
    params = pltpu.CompilerParams(vmem_limit_bytes=8 * 1024 * 1024)

    down2 = exchange(adapter_down_weight, 1, devices)
    up2 = exchange(adapter_up_weight, 1, devices)
    extent = adapter_down_weight.shape[0]
    mask = pl.pallas_call(
        functools.partial(mask_kernel, rows, extent),
        out_shape=jax.ShapeDtypeStruct((half, 2 * extent), jnp.float32),
        in_specs=[smem] * 3,
        out_specs=vmem,
        compiler_params=params,
        name="mask",
    )(request_adapter[:, 0], adapter_block_count, adapter_store_slot)
    near, weight = load(tokens, base_projection_weight)
    first = tokens
    down, up = adapter_down_weight, adapter_up_weight
    for k, stage in enumerate(stages_of(devices)):
        got = [exchange(first if k == 0 else near, m, devices) for m in stage]
        if k == 1:
            down, up, near = lax.optimization_barrier((down, up, near))
            down, up = load(down, up)
            down, up, near, got, mask = lax.optimization_barrier((down, up, near, got, mask))
        if k == 0:
            near, weight, got = lax.optimization_barrier((near, weight, got))
        near = jnp.concatenate([near] + got, axis=0)
    far = exchange(near, 1, devices)

    delta = pl.pallas_call(
        functools.partial(delta_kernel, rows),
        out_shape=jax.ShapeDtypeStruct((half, model), jnp.bfloat16),
        in_specs=[vmem] * 6,
        out_specs=vmem,
        compiler_params=params,
        name="delta",
    )(
        mask,
        near,
        down,
        down2,
        up,
        up2,
    )
    base, far_base = pl.pallas_call(
        base_kernel,
        out_shape=[jax.ShapeDtypeStruct((half, weight.shape[1]), jnp.float32)] * 2,
        in_specs=[vmem] * 3,
        out_specs=[vmem] * 2,
        compiler_params=params,
        name="base",
    )(near, far, weight)
    base2 = exchange(far_base, 1, devices)
    summed = pl.pallas_call(
        functools.partial(add_kernel, rows),
        out_shape=jax.ShapeDtypeStruct((half, model), jnp.bfloat16),
        in_specs=[vmem] * 3,
        out_specs=vmem,
        compiler_params=params,
        name="add",
    )(delta, base, base2)
    summed = summed.reshape(devices // 2, rows, model)
    groups = [[d for d in range(devices) if d % 2 == c] for c in (0, 1)]
    pieces = lax.all_to_all(summed, "pool", 0, 0, tiled=True, axis_index_groups=groups)
    return jnp.sum(pieces.astype(jnp.float32), axis=0).astype(jnp.bfloat16)


def solution(mesh):
    return jax.shard_map(
        body,
        mesh=mesh,
        in_specs=(
            P(("groups", "pool"), None),
            P(None, "pool"),
            P("pool", None),
            P("pool", None),
            P("groups", None),
            P(),
            P(),
        ),
        out_specs=P(("groups", "pool"), None),
        check_vma=False,
    )
```

```python
import functools

import jax
import jax.numpy as jnp
from jax import lax
from jax.experimental import pallas as pl
from jax.experimental.pallas import tpu as pltpu
from jax.sharding import PartitionSpec as P

RANK_BLOCK = 16
LANES = 128
SPACE = pltpu.HBM


def stages_of(devices):
    bits = [1 << k for k in range(1, devices.bit_length() - 1)]
    stages = [[b] for b in bits[:1]]
    rest = bits[1:]
    for k in range(0, len(rest), 2):
        low = rest[k]
        stages.append([low, rest[k + 1], low + rest[k + 1]] if k + 1 < len(rest) else [low])
    return stages


def exchange(array, mask, devices):
    return lax.ppermute(array, "pool", [(d, d ^ mask) for d in range(devices)])


def canonical(rows, half, device):
    to = lax.broadcasted_iota(jnp.int32, (half, half), 0)
    of = lax.broadcasted_iota(jnp.int32, (half, half), 1)
    return to == (of ^ (rows * (device // 2)))


def mask_kernel(rows, extent, ident_ref, count_ref, slot_ref, out_ref):
    half = out_ref.shape[0]
    device = lax.axis_index("pool")

    def ranks(a, held):
        slot, count = slot_ref[a], count_ref[a] * RANK_BLOCK
        return jnp.where(slot == device, count, held[0]), jnp.where(slot == device ^ 1, count, held[1])

    rank, rank2 = lax.fori_loop(0, slot_ref.shape[0], ranks, (jnp.int32(0), jnp.int32(0)))
    row = lax.broadcasted_iota(jnp.int32, out_ref.shape, 0)
    col = lax.broadcasted_iota(jnp.int32, out_ref.shape, 1)

    def limits(q, held):
        request = (q // rows * 2 + device % 2) * rows + q % rows
        slot = slot_ref[ident_ref[request]]
        low = jnp.where(slot == device ^ 1, extent, 0)
        high = jnp.where(slot == device, rank, jnp.where(slot == device ^ 1, extent + rank2, 0))
        return jnp.where((row == q) & (col >= low) & (col < high), 1.0, held)

    out_ref[...] = lax.fori_loop(0, half, limits, jnp.zeros(out_ref.shape, jnp.float32), unroll=min(half, 16))


def shrink_kernel(rows, mask_ref, near_ref, down_ref, down2_ref, out_ref):
    half, extent = near_ref.shape[0], down_ref.shape[0]
    order = canonical(rows, half, lax.axis_index("pool")).astype(jnp.bfloat16)
    near = near_ref[...]
    shrink = jnp.concatenate(
        [
            lax.dot_general(near, ref[...], (((1,), (1,)), ((), ())), preferred_element_type=jnp.float32)
            for ref in (down_ref, down2_ref)
        ],
        axis=1,
    )
    shrink = jnp.dot(order, shrink.astype(jnp.bfloat16), preferred_element_type=jnp.float32)
    out_ref[...] = jnp.where(mask_ref[...] > 0, shrink, 0.0).astype(jnp.bfloat16)


def delta_kernel(shrink_ref, up_ref, up2_ref, out_ref):
    extent, model = up_ref.shape
    step = min(1024, model)
    for c in range(0, model, step):
        span = slice(c, c + step)
        out_ref[:, span] = (
            jnp.dot(shrink_ref[:, :extent], up_ref[:, span], preferred_element_type=jnp.float32)
            + jnp.dot(shrink_ref[:, extent:], up2_ref[:, span], preferred_element_type=jnp.float32)
        ).astype(jnp.bfloat16)


def base_kernel(near_ref, far_ref, weight_ref, near_out, far_out):
    half = near_ref.shape[0]
    x = jnp.concatenate([near_ref[...], far_ref[...]], axis=0)
    base = jnp.dot(x, weight_ref[...], preferred_element_type=jnp.float32)
    near_out[...] = base[:half]
    far_out[...] = base[half:]


def load_kernel(count, *refs):
    copies = [
        pltpu.make_async_copy(refs[i], refs[count + i], refs[2 * count].at[i]) for i in range(count)
    ]
    for copy in copies:
        copy.start()
    for copy in copies:
        copy.wait()


def load(*arrays):
    count = len(arrays)
    return pl.pallas_call(
        functools.partial(load_kernel, count),
        out_shape=[pltpu.VMEM(a.shape, a.dtype) for a in arrays],
        in_specs=[pl.BlockSpec(memory_space=SPACE)] * count,
        out_specs=[pl.BlockSpec(memory_space=pltpu.VMEM)] * count,
        scratch_shapes=[pltpu.SemaphoreType.DMA((count,))],
        cost_estimate=pl.CostEstimate(
            flops=0, bytes_accessed=sum(2 * a.size * a.dtype.itemsize for a in arrays), transcendentals=0
        ),
        compiler_params=pltpu.CompilerParams(vmem_limit_bytes=1024 * 1024),
        name="load",
    )(*[pltpu.with_memory_space_constraint(a, pltpu.HBM) for a in arrays])


def add_kernel(rows, delta_ref, base_ref, base2_ref, out_ref):
    half, width = base_ref.shape
    device = lax.axis_index("pool")
    order = canonical(rows, half, device).astype(jnp.float32)
    placed = [
        jnp.dot(order, ref[...], preferred_element_type=jnp.float32, precision=lax.Precision.HIGHEST)
        for ref in (base_ref, base2_ref)
    ]
    odd = device % 2 == 1
    both = jnp.concatenate(
        [jnp.where(odd, placed[1], placed[0]), jnp.where(odd, placed[0], placed[1])], axis=1
    )
    wide = 2 * width
    lanes = max(wide, LANES)
    columns = pl.ds(pl.multiple_of(device // 2 * wide // lanes * lanes, lanes), lanes)
    lane = lax.broadcasted_iota(jnp.int32, (half, lanes), 1)
    inside = lane // wide == device // 2 % (lanes // wide)
    both = jnp.where(inside, jnp.concatenate([both] * (lanes // wide), axis=1), 0.0)
    out_ref[...] = delta_ref[...]
    out_ref[:, columns] = (both + delta_ref[:, columns].astype(jnp.float32)).astype(jnp.bfloat16)


def body(
    tokens,
    base_projection_weight,
    adapter_down_weight,
    adapter_up_weight,
    request_adapter,
    adapter_block_count,
    adapter_store_slot,
):
    devices = lax.axis_size("pool")
    rows, model = tokens.shape
    half = devices // 2 * rows
    vmem, smem = pl.BlockSpec(memory_space=pltpu.VMEM), pl.BlockSpec(memory_space=pltpu.SMEM)
    params = pltpu.CompilerParams(vmem_limit_bytes=8 * 1024 * 1024)

    down2 = exchange(adapter_down_weight, 1, devices)
    up2 = exchange(adapter_up_weight, 1, devices)
    extent = adapter_down_weight.shape[0]
    mask = pl.pallas_call(
        functools.partial(mask_kernel, rows, extent),
        out_shape=jax.ShapeDtypeStruct((half, 2 * extent), jnp.float32),
        in_specs=[smem] * 3,
        out_specs=vmem,
        compiler_params=params,
        name="mask",
    )(request_adapter[:, 0], adapter_block_count, adapter_store_slot)
    near, weight = load(tokens, base_projection_weight)
    first = tokens
    down, up = adapter_down_weight, adapter_up_weight
    for k, stage in enumerate(stages_of(devices)):
        got = [exchange(first if k == 0 else near, m, devices) for m in stage[::-1]][::-1]
        if k == 1:
            down, up, near = lax.optimization_barrier((down, up, near))
            down, up = load(down, up)
            down, up, near, got, mask = lax.optimization_barrier((down, up, near, got, mask))
        if k == 0:
            near, weight, got = lax.optimization_barrier((near, weight, got))
        near = jnp.concatenate([near] + got, axis=0)
    far = exchange(near, 1, devices)

    shrink = pl.pallas_call(
        functools.partial(shrink_kernel, rows),
        out_shape=jax.ShapeDtypeStruct((half, 2 * extent), jnp.bfloat16),
        in_specs=[vmem] * 4,
        out_specs=vmem,
        compiler_params=params,
        name="shrink",
    )(mask, near, down, down2)
    far, shrink = lax.optimization_barrier((far, shrink))
    base, far_base = pl.pallas_call(
        base_kernel,
        out_shape=[jax.ShapeDtypeStruct((half, weight.shape[1]), jnp.float32)] * 2,
        in_specs=[vmem] * 3,
        out_specs=[vmem] * 2,
        compiler_params=params,
        name="base",
    )(near, far, weight)
    shrink, base, far_base = lax.optimization_barrier((shrink, base, far_base))
    base2 = exchange(far_base, 1, devices)
    delta = pl.pallas_call(
        delta_kernel,
        out_shape=jax.ShapeDtypeStruct((half, model), jnp.bfloat16),
        in_specs=[vmem] * 3,
        out_specs=vmem,
        compiler_params=params,
        name="delta",
    )(shrink, up, up2)
    summed = pl.pallas_call(
        functools.partial(add_kernel, rows),
        out_shape=jax.ShapeDtypeStruct((half, model), jnp.bfloat16),
        in_specs=[vmem] * 3,
        out_specs=vmem,
        compiler_params=params,
        name="add",
    )(delta, base, base2)
    summed = summed.reshape(devices // 2, rows, model)
    groups = [[d for d in range(devices) if d % 2 == c] for c in (0, 1)]
    pieces = lax.all_to_all(summed, "pool", 0, 0, tiled=True, axis_index_groups=groups)
    return jnp.sum(pieces.astype(jnp.float32), axis=0).astype(jnp.bfloat16)


def solution(mesh):
    return jax.shard_map(
        body,
        mesh=mesh,
        in_specs=(
            P(("groups", "pool"), None),
            P(None, "pool"),
            P("pool", None),
            P("pool", None),
            P("groups", None),
            P(),
            P(),
        ),
        out_specs=P(("groups", "pool"), None),
        check_vma=False,
    )
```

```python
import functools

import jax
import jax.numpy as jnp
from jax import lax
from jax.experimental import pallas as pl
from jax.experimental.pallas import tpu as pltpu
from jax.sharding import PartitionSpec as P

RANK_BLOCK = 16
LANES = 128


def stages_of(devices):
    bits = [1 << k for k in range(1, devices.bit_length() - 1)]
    stages = [[b] for b in bits[:1]]
    rest = bits[1:]
    for k in range(0, len(rest), 2):
        low = rest[k]
        stages.append([low, rest[k + 1], low + rest[k + 1]] if k + 1 < len(rest) else [low])
    return stages


def exchange(array, mask, devices):
    return lax.ppermute(array, "pool", [(d, d ^ mask) for d in range(devices)])


def canonical(rows, half, device):
    to = lax.broadcasted_iota(jnp.int32, (half, half), 0)
    of = lax.broadcasted_iota(jnp.int32, (half, half), 1)
    return to == (of ^ (rows * (device // 2)))


def mask_kernel(rows, extent, ident_ref, count_ref, slot_ref, out_ref):
    half = out_ref.shape[0]
    device = lax.axis_index("pool")

    def ranks(a, held):
        slot, count = slot_ref[a], count_ref[a] * RANK_BLOCK
        return jnp.where(slot == device, count, held[0]), jnp.where(slot == device ^ 1, count, held[1])

    adapters = slot_ref.shape[0]
    rank, rank2 = lax.fori_loop(
        0, adapters, ranks, (jnp.int32(0), jnp.int32(0)), unroll=min(adapters, 16)
    )
    row = lax.broadcasted_iota(jnp.int32, out_ref.shape, 0)
    col = lax.broadcasted_iota(jnp.int32, out_ref.shape, 1)

    def limits(q, held):
        request = (q // rows * 2 + device % 2) * rows + q % rows
        slot = slot_ref[ident_ref[request]]
        low = jnp.where(slot == device ^ 1, extent, 0)
        high = jnp.where(slot == device, rank, jnp.where(slot == device ^ 1, extent + rank2, 0))
        return jnp.where((row == q) & (col >= low) & (col < high), 1.0, held)

    out_ref[...] = lax.fori_loop(0, half, limits, jnp.zeros(out_ref.shape, jnp.float32), unroll=min(half, 16))


def shrink_kernel(rows, mask_ref, near_ref, down_ref, down2_ref, out_ref):
    half, extent = near_ref.shape[0], down_ref.shape[0]
    order = canonical(rows, half, lax.axis_index("pool")).astype(jnp.bfloat16)
    near = near_ref[...]
    shrink = jnp.concatenate(
        [
            lax.dot_general(near, ref[...], (((1,), (1,)), ((), ())), preferred_element_type=jnp.float32)
            for ref in (down_ref, down2_ref)
        ],
        axis=1,
    )
    shrink = jnp.dot(order, shrink.astype(jnp.bfloat16), preferred_element_type=jnp.float32)
    out_ref[...] = jnp.where(mask_ref[...] > 0, shrink, 0.0).astype(jnp.bfloat16)


def delta_kernel(shrink_ref, up_ref, up2_ref, out_ref):
    extent, model = up_ref.shape
    step = min(1024, model)
    for c in range(0, model, step):
        span = slice(c, c + step)
        out_ref[:, span] = (
            jnp.dot(shrink_ref[:, :extent], up_ref[:, span], preferred_element_type=jnp.float32)
            + jnp.dot(shrink_ref[:, extent:], up2_ref[:, span], preferred_element_type=jnp.float32)
        ).astype(jnp.bfloat16)


def base_kernel(near_ref, far_ref, weight_ref, weight2_ref, near_out, far_out):
    half = near_ref.shape[0]
    cut = weight_ref.shape[0]
    x = jnp.concatenate([near_ref[...], far_ref[...]], axis=0)
    base = jnp.dot(x[:, :cut], weight_ref[...], preferred_element_type=jnp.float32)
    base += jnp.dot(x[:, cut:], weight2_ref[...], preferred_element_type=jnp.float32)
    near_out[...] = base[:half]
    far_out[...] = base[half:]


def load_kernel(starts, *refs):
    count = len(starts)
    copies = []
    for i, start in enumerate(starts):
        held = refs[count + i]
        source = refs[i].at[pl.ds(start, held.shape[0])]
        copies.append(pltpu.make_async_copy(source, held, refs[2 * count].at[i]))
    for copy in copies:
        copy.start()
    for copy in copies:
        copy.wait()


def load(*parts):
    count = len(parts)
    shapes = [((stop - start, a.shape[1]), a.dtype) for a, start, stop in parts]
    return pl.pallas_call(
        functools.partial(load_kernel, [start for _, start, _ in parts]),
        out_shape=[pltpu.VMEM(*shape) for shape in shapes],
        in_specs=[pl.BlockSpec(memory_space=pltpu.HBM)] * count,
        out_specs=[pl.BlockSpec(memory_space=pltpu.VMEM)] * count,
        scratch_shapes=[pltpu.SemaphoreType.DMA((count,))],
        cost_estimate=pl.CostEstimate(
            flops=0, bytes_accessed=sum(4 * dims[0] * dims[1] for dims, _ in shapes), transcendentals=0
        ),
        compiler_params=pltpu.CompilerParams(vmem_limit_bytes=1024 * 1024),
        name="load",
    )(*[pltpu.with_memory_space_constraint(a, pltpu.HBM) for a, _, _ in parts])


def add_kernel(rows, delta_ref, base_ref, base2_ref, out_ref):
    half, width = base_ref.shape
    device = lax.axis_index("pool")
    order = canonical(rows, half, device).astype(jnp.float32)
    placed = [
        jnp.dot(order, ref[...], preferred_element_type=jnp.float32, precision=lax.Precision.HIGHEST)
        for ref in (base_ref, base2_ref)
    ]
    odd = device % 2 == 1
    both = jnp.concatenate(
        [jnp.where(odd, placed[1], placed[0]), jnp.where(odd, placed[0], placed[1])], axis=1
    )
    wide = 2 * width
    lanes = max(wide, LANES)
    columns = pl.ds(pl.multiple_of(device // 2 * wide // lanes * lanes, lanes), lanes)
    lane = lax.broadcasted_iota(jnp.int32, (half, lanes), 1)
    inside = lane // wide == device // 2 % (lanes // wide)
    both = jnp.where(inside, jnp.concatenate([both] * (lanes // wide), axis=1), 0.0)
    out_ref[...] = delta_ref[...].reshape(out_ref.shape)
    both = (both + delta_ref[:, columns].astype(jnp.float32)).astype(jnp.bfloat16)
    out_ref[:, :, columns] = both.reshape(out_ref.shape[:2] + (lanes,))


def sum_kernel(pieces_ref, out_ref):
    out_ref[...] = jnp.sum(pieces_ref[...].astype(jnp.float32), axis=0).astype(jnp.bfloat16)


def body(
    tokens,
    base_projection_weight,
    adapter_down_weight,
    adapter_up_weight,
    request_adapter,
    adapter_block_count,
    adapter_store_slot,
):
    devices = lax.axis_size("pool")
    rows, model = tokens.shape
    half = devices // 2 * rows
    vmem, smem = pl.BlockSpec(memory_space=pltpu.VMEM), pl.BlockSpec(memory_space=pltpu.SMEM)
    params = pltpu.CompilerParams(vmem_limit_bytes=8 * 1024 * 1024)

    down2 = exchange(adapter_down_weight, 1, devices)
    up2 = exchange(adapter_up_weight, 1, devices)
    extent = adapter_down_weight.shape[0]
    mask = pl.pallas_call(
        functools.partial(mask_kernel, rows, extent),
        out_shape=jax.ShapeDtypeStruct((half, 2 * extent), jnp.float32),
        in_specs=[smem] * 3,
        out_specs=vmem,
        compiler_params=params,
        name="mask",
    )(request_adapter[:, 0], adapter_block_count, adapter_store_slot)
    weight, down, up = base_projection_weight, adapter_down_weight, adapter_up_weight
    cut = model * 3 // 8
    near, head = load((tokens, 0, rows), (weight, 0, cut))
    for k, stage in enumerate(stages_of(devices)):
        got = [exchange(near if k else tokens, m, devices) for m in stage]
        if k == 0:
            near, head, got = lax.optimization_barrier((near, head, got))
        if k == 1:
            weight, down, up, near = lax.optimization_barrier((weight, down, up, near))
            (tail,) = load((weight, cut, model))
            near, tail, mask, *got = lax.optimization_barrier((near, tail, mask, *got[::-1]))
            got = got[::-1]
        near = jnp.concatenate([near] + got, axis=0)
    far = exchange(near, 1, devices)

    shrink = pl.pallas_call(
        functools.partial(shrink_kernel, rows),
        out_shape=jax.ShapeDtypeStruct((half, 2 * extent), jnp.bfloat16),
        in_specs=[vmem] * 4,
        out_specs=vmem,
        compiler_params=params,
        name="shrink",
    )(mask, near, down, down2)
    far, shrink = lax.optimization_barrier((far, shrink))
    base, far_base = pl.pallas_call(
        base_kernel,
        out_shape=[jax.ShapeDtypeStruct((half, weight.shape[1]), jnp.float32)] * 2,
        in_specs=[vmem] * 4,
        out_specs=[vmem] * 2,
        compiler_params=params,
        name="base",
    )(near, far, head, tail)
    shrink, base, far_base = lax.optimization_barrier((shrink, base, far_base))
    base2 = exchange(far_base, 1, devices)
    delta = pl.pallas_call(
        delta_kernel,
        out_shape=jax.ShapeDtypeStruct((half, model), jnp.bfloat16),
        in_specs=[vmem] * 3,
        out_specs=vmem,
        compiler_params=params,
        name="delta",
    )(shrink, up, up2)
    summed = pl.pallas_call(
        functools.partial(add_kernel, rows),
        out_shape=pltpu.VMEM((devices // 2, rows, model), jnp.bfloat16),
        in_specs=[vmem] * 3,
        out_specs=vmem,
        compiler_params=params,
        name="add",
    )(delta, base, base2)
    groups = [[d for d in range(devices) if d % 2 == c] for c in (0, 1)]
    pieces = lax.all_to_all(summed, "pool", 0, 0, tiled=True, axis_index_groups=groups)
    return pl.pallas_call(
        sum_kernel,
        out_shape=jax.ShapeDtypeStruct((rows, model), jnp.bfloat16),
        in_specs=[vmem],
        out_specs=vmem,
        compiler_params=params,
        name="sum",
    )(pieces)


def solution(mesh):
    return jax.shard_map(
        body,
        mesh=mesh,
        in_specs=(
            P(("groups", "pool"), None),
            P(None, "pool"),
            P("pool", None),
            P("pool", None),
            P("groups", None),
            P(),
            P(),
        ),
        out_specs=P(("groups", "pool"), None),
        check_vma=False,
    )
```

```python
import functools

import jax
import jax.numpy as jnp
from jax import lax
from jax.experimental import pallas as pl
from jax.experimental.pallas import tpu as pltpu
from jax.sharding import PartitionSpec as P

RANK_BLOCK = 16
LANES = 128


def stages_of(devices):
    bits = [1 << k for k in range(1, devices.bit_length() - 1)]
    stages = [[b] for b in bits[:1]]
    rest = bits[1:]
    for k in range(0, len(rest), 2):
        low = rest[k]
        stages.append([low, rest[k + 1], low + rest[k + 1]] if k + 1 < len(rest) else [low])
    return stages


def exchange(array, mask, devices):
    return lax.ppermute(array, "pool", [(d, d ^ mask) for d in range(devices)])


def by_y(rows, half):
    to = lax.broadcasted_iota(jnp.int32, (half, half), 0)
    of = lax.broadcasted_iota(jnp.int32, (half, half), 1)
    return of == to % (half // 2) // rows * 2 * rows + to // (half // 2) * rows + to % rows


def mask_kernel(rows, extent, ident_ref, count_ref, slot_ref, out_ref):
    half = out_ref.shape[0]
    device = lax.axis_index("pool")

    def ranks(a, held):
        slot, count = slot_ref[a], count_ref[a] * RANK_BLOCK
        return jnp.where(slot == device, count, held[0]), jnp.where(slot == device ^ 1, count, held[1])

    adapters = slot_ref.shape[0]
    rank, rank2 = lax.fori_loop(
        0, adapters, ranks, (jnp.int32(0), jnp.int32(0)), unroll=min(adapters, 16)
    )
    row = lax.broadcasted_iota(jnp.int32, out_ref.shape, 0)
    col = lax.broadcasted_iota(jnp.int32, out_ref.shape, 1)

    def limits(q, held):
        chip = q % (half // 2) // rows * 2 + q // (half // 2)
        request = (device ^ (2 * chip)) * rows + q % rows
        slot = slot_ref[ident_ref[request]]
        low = jnp.where(slot == device ^ 1, extent, 0)
        high = jnp.where(slot == device, rank, jnp.where(slot == device ^ 1, extent + rank2, 0))
        return jnp.where((row == q) & (col >= low) & (col < high), 1.0, held)

    out_ref[...] = lax.fori_loop(0, half, limits, jnp.zeros(out_ref.shape, jnp.float32), unroll=min(half, 16))


def shrink_kernel(rows, mask_ref, near_ref, down_ref, down2_ref, out_ref):
    near = near_ref[...]
    shrink = jnp.concatenate(
        [
            lax.dot_general(near, ref[...], (((1,), (1,)), ((), ())), preferred_element_type=jnp.float32)
            for ref in (down_ref, down2_ref)
        ],
        axis=1,
    )
    order = by_y(rows, near.shape[0]).astype(jnp.bfloat16)
    shrink = jnp.dot(order, shrink.astype(jnp.bfloat16), preferred_element_type=jnp.float32)
    out_ref[...] = jnp.where(mask_ref[...] > 0, shrink, 0.0).astype(jnp.bfloat16)


def delta_kernel(shrink_ref, up_ref, up2_ref, own_out, other_out):
    extent, model = up_ref.shape
    part = own_out.shape[0]
    step = min(1024, model)
    for c in range(0, model, step):
        span = slice(c, c + step)
        delta = jnp.dot(
            shrink_ref[:, :extent], up_ref[:, span], preferred_element_type=jnp.float32
        ) + jnp.dot(shrink_ref[:, extent:], up2_ref[:, span], preferred_element_type=jnp.float32)
        own_out[:, span] = delta[:part].astype(jnp.bfloat16)
        other_out[:, span] = delta[part:].astype(jnp.bfloat16)


def base_kernel(rows, near_ref, far_ref, weight_ref, weight2_ref, *outs):
    part = outs[0].shape[0]
    cut = weight_ref.shape[0]
    x = jnp.concatenate([near_ref[...], far_ref[...]], axis=0)
    base = jnp.dot(x[:, :cut], weight_ref[...], preferred_element_type=jnp.float32)
    base += jnp.dot(x[:, cut:], weight2_ref[...], preferred_element_type=jnp.float32)
    order = by_y(rows, 2 * part).astype(jnp.float32)
    for k in (0, 2):
        placed = jnp.dot(
            order,
            base[k * part : (k + 2) * part],
            preferred_element_type=jnp.float32,
            precision=lax.Precision.HIGHEST,
        )
        outs[k][...] = placed[:part]
        outs[k + 1][...] = placed[part:]


def load_kernel(starts, *refs):
    count = len(starts)
    copies = []
    for i, start in enumerate(starts):
        held = refs[count + i]
        source = refs[i].at[pl.ds(start, held.shape[0])]
        copies.append(pltpu.make_async_copy(source, held, refs[2 * count].at[i]))
    for copy in copies:
        copy.start()
    for copy in copies:
        copy.wait()


def load(*parts):
    count = len(parts)
    shapes = [((stop - start, a.shape[1]), a.dtype) for a, start, stop in parts]
    return pl.pallas_call(
        functools.partial(load_kernel, [start for _, start, _ in parts]),
        out_shape=[pltpu.VMEM(*shape) for shape in shapes],
        in_specs=[pl.BlockSpec(memory_space=pltpu.HBM)] * count,
        out_specs=[pl.BlockSpec(memory_space=pltpu.VMEM)] * count,
        scratch_shapes=[pltpu.SemaphoreType.DMA((count,))],
        cost_estimate=pl.CostEstimate(
            flops=0, bytes_accessed=sum(4 * dims[0] * dims[1] for dims, _ in shapes), transcendentals=0
        ),
        compiler_params=pltpu.CompilerParams(vmem_limit_bytes=1024 * 1024),
        name="load",
    )(*[pltpu.with_memory_space_constraint(a, pltpu.HBM) for a, _, _ in parts])


def add_kernel(own_ref, other_ref, *refs):
    pieces, outs = [refs[k][...] for k in (0, 3, 1, 2)], refs[4:]
    rows = outs[0].shape[0]
    width = pieces[0].shape[1]
    device = lax.axis_index("pool")
    columns = pl.ds(pl.multiple_of(device // 4 * (4 * width), 4 * width), 4 * width)
    base = []
    for place in range(4):
        piece = pieces[0]
        for mask in (1, 2, 3):
            piece = jnp.where(device % 4 == place ^ mask, pieces[mask], piece)
        base.append(piece)
    base = jnp.concatenate(base, axis=1)
    both = own_ref[...].astype(jnp.float32) + other_ref[...].astype(jnp.float32)
    part = own_ref[:, columns].astype(jnp.float32) + other_ref[:, columns].astype(jnp.float32) + base
    for k, out in enumerate(outs):
        span = slice(k * rows, (k + 1) * rows)
        out[...] = both[span].astype(jnp.bfloat16)
        out[:, columns] = part[span].astype(jnp.bfloat16)


def sum_kernel(*refs):
    total = refs[0][...].astype(jnp.float32)
    for ref in refs[1:-1]:
        total += ref[...].astype(jnp.float32)
    refs[-1][...] = total.astype(jnp.bfloat16)


def body(
    tokens,
    base_projection_weight,
    adapter_down_weight,
    adapter_up_weight,
    request_adapter,
    adapter_block_count,
    adapter_store_slot,
):
    devices = lax.axis_size("pool")
    rows, model = tokens.shape
    half = devices // 2 * rows
    vmem, smem = pl.BlockSpec(memory_space=pltpu.VMEM), pl.BlockSpec(memory_space=pltpu.SMEM)
    params = pltpu.CompilerParams(vmem_limit_bytes=8 * 1024 * 1024)

    down2 = exchange(adapter_down_weight, 1, devices)
    up2 = exchange(adapter_up_weight, 1, devices)
    extent = adapter_down_weight.shape[0]
    mask = pl.pallas_call(
        functools.partial(mask_kernel, rows, extent),
        out_shape=jax.ShapeDtypeStruct((half, 2 * extent), jnp.float32),
        in_specs=[smem] * 3,
        out_specs=vmem,
        compiler_params=params,
        name="mask",
    )(request_adapter[:, 0], adapter_block_count, adapter_store_slot)
    weight, down, up = base_projection_weight, adapter_down_weight, adapter_up_weight
    cut = model // 2
    near, head = load((tokens, 0, rows), (weight, 0, cut))
    for k, stage in enumerate(stages_of(devices)):
        got = [exchange(near if k else tokens, m, devices) for m in stage]
        if k == 0:
            near, head, got = lax.optimization_barrier((near, head, got))
        if k == 1:
            weight, down, up, near = lax.optimization_barrier((weight, down, up, near))
            (tail,) = load((weight, cut, model))
            near, tail, mask, *got = lax.optimization_barrier((near, tail, mask, *got[::-1]))
            got = got[::-1]
        near = jnp.concatenate([near] + got, axis=0)
    far = exchange(near, 1, devices)

    shrink = pl.pallas_call(
        functools.partial(shrink_kernel, rows),
        out_shape=jax.ShapeDtypeStruct((half, 2 * extent), jnp.bfloat16),
        in_specs=[vmem] * 4,
        out_specs=vmem,
        compiler_params=params,
        name="shrink",
    )(mask, near, down, down2)
    own, other = pl.pallas_call(
        delta_kernel,
        out_shape=[jax.ShapeDtypeStruct((half // 2, model), jnp.bfloat16)] * 2,
        in_specs=[vmem] * 3,
        out_specs=[vmem] * 2,
        compiler_params=params,
        name="delta",
    )(shrink, up, up2)
    other = exchange(other, 2, devices)
    far, own = lax.optimization_barrier((far, own))
    base = pl.pallas_call(
        functools.partial(base_kernel, rows),
        out_shape=[jax.ShapeDtypeStruct((half // 2, weight.shape[1]), jnp.float32)] * 4,
        in_specs=[vmem] * 4,
        out_specs=[vmem] * 4,
        compiler_params=params,
        name="base",
    )(near, far, head, tail)
    base = [base[0], exchange(base[2], 1, devices), exchange(base[1], 2, devices), exchange(base[3], 3, devices)]
    sums = pl.pallas_call(
        add_kernel,
        out_shape=[jax.ShapeDtypeStruct((rows, model), jnp.bfloat16)] * (devices // 4),
        in_specs=[vmem] * 6,
        out_specs=[vmem] * (devices // 4),
        compiler_params=params,
        name="add",
    )(own, other, base[0], base[2], base[3], base[1])
    got = [exchange(sums[k], 4 * k, devices) for k in range(1, devices // 4)]
    return pl.pallas_call(
        sum_kernel,
        out_shape=jax.ShapeDtypeStruct((rows, model), jnp.bfloat16),
        in_specs=[vmem] * (devices // 4),
        out_specs=vmem,
        compiler_params=params,
        name="sum",
    )(sums[0], *got[::-1])


def solution(mesh):
    return jax.shard_map(
        body,
        mesh=mesh,
        in_specs=(
            P(("groups", "pool"), None),
            P(None, "pool"),
            P("pool", None),
            P("pool", None),
            P("groups", None),
            P(),
            P(),
        ),
        out_specs=P(("groups", "pool"), None),
        check_vma=False,
    )
```

```python
import functools

import jax
import jax.numpy as jnp
from jax import lax
from jax.experimental import pallas as pl
from jax.experimental.pallas import tpu as pltpu
from jax.sharding import PartitionSpec as P

RANK_BLOCK = 16
LANES = 128


def stages_of(devices):
    bits = [1 << k for k in range(1, devices.bit_length() - 1)]
    stages = [[b] for b in bits[:1]]
    rest = bits[1:]
    for k in range(0, len(rest), 2):
        low = rest[k]
        stages.append([low, rest[k + 1], low + rest[k + 1]] if k + 1 < len(rest) else [low])
    return stages


def exchange(array, mask, devices):
    return lax.ppermute(array, "pool", [(d, d ^ mask) for d in range(devices)])


def by_y(rows, array):
    blocks = [array[r : r + rows] for r in range(0, array.shape[0], rows)]
    return jnp.concatenate(blocks[::2] + blocks[1::2], axis=0)


def mask_kernel(rows, extent, ident_ref, count_ref, slot_ref, out_ref):
    half = out_ref.shape[0]
    device = lax.axis_index("pool")

    def ranks(a, held):
        slot, count = slot_ref[a], count_ref[a] * RANK_BLOCK
        return jnp.where(slot == device, count, held[0]), jnp.where(slot == device ^ 1, count, held[1])

    adapters = slot_ref.shape[0]
    rank, rank2 = lax.fori_loop(
        0, adapters, ranks, (jnp.int32(0), jnp.int32(0)), unroll=min(adapters, 16)
    )
    row = lax.broadcasted_iota(jnp.int32, out_ref.shape, 0)
    col = lax.broadcasted_iota(jnp.int32, out_ref.shape, 1)

    def limits(q, held):
        chip = q % (half // 2) // rows * 2 + q // (half // 2)
        request = (device ^ (2 * chip)) * rows + q % rows
        slot = slot_ref[ident_ref[request]]
        low = jnp.where(slot == device ^ 1, extent, 0)
        high = jnp.where(slot == device, rank, jnp.where(slot == device ^ 1, extent + rank2, 0))
        return jnp.where((row == q) & (col >= low) & (col < high), 1.0, held)

    out_ref[...] = lax.fori_loop(0, half, limits, jnp.zeros(out_ref.shape, jnp.float32), unroll=min(half, 16))


def shrink_kernel(rows, mask_ref, near_ref, down_ref, down2_ref, out_ref):
    near = near_ref[...]
    shrink = jnp.concatenate(
        [
            lax.dot_general(near, ref[...], (((1,), (1,)), ((), ())), preferred_element_type=jnp.float32)
            for ref in (down_ref, down2_ref)
        ],
        axis=1,
    )
    out_ref[...] = jnp.where(mask_ref[...] > 0, by_y(rows, shrink), 0.0).astype(jnp.bfloat16)


def delta_kernel(shrink_ref, up_ref, up2_ref, own_out, other_out):
    extent, model = up_ref.shape
    part = own_out.shape[0]
    step = min(1024, model)
    for c in range(0, model, step):
        span = slice(c, c + step)
        delta = jnp.dot(
            shrink_ref[:, :extent], up_ref[:, span], preferred_element_type=jnp.float32
        ) + jnp.dot(shrink_ref[:, extent:], up2_ref[:, span], preferred_element_type=jnp.float32)
        own_out[:, span] = delta[:part].astype(jnp.bfloat16)
        other_out[:, span] = delta[part:].astype(jnp.bfloat16)


def base_kernel(rows, near_ref, far_ref, weight_ref, weight2_ref, *outs):
    part = outs[0].shape[0]
    cut = weight_ref.shape[0]
    x = jnp.concatenate([near_ref[...], far_ref[...]], axis=0)
    base = jnp.dot(x[:, :cut], weight_ref[...], preferred_element_type=jnp.float32)
    base += jnp.dot(x[:, cut:], weight2_ref[...], preferred_element_type=jnp.float32)
    for k in (0, 2):
        placed = by_y(rows, base[k * part : (k + 2) * part])
        outs[k][...] = placed[:part]
        outs[k + 1][...] = placed[part:]


def load_kernel(starts, *refs):
    count = len(starts)
    copies = []
    for i, start in enumerate(starts):
        held = refs[count + i]
        source = refs[i].at[pl.ds(start, held.shape[0])]
        copies.append(pltpu.make_async_copy(source, held, refs[2 * count].at[i]))
    for copy in copies:
        copy.start()
    for copy in copies:
        copy.wait()


def load(*parts):
    count = len(parts)
    shapes = [((stop - start, a.shape[1]), a.dtype) for a, start, stop in parts]
    return pl.pallas_call(
        functools.partial(load_kernel, [start for _, start, _ in parts]),
        out_shape=[pltpu.VMEM(*shape) for shape in shapes],
        in_specs=[pl.BlockSpec(memory_space=pltpu.HBM)] * count,
        out_specs=[pl.BlockSpec(memory_space=pltpu.VMEM)] * count,
        scratch_shapes=[pltpu.SemaphoreType.DMA((count,))],
        cost_estimate=pl.CostEstimate(
            flops=0, bytes_accessed=sum(4 * dims[0] * dims[1] for dims, _ in shapes), transcendentals=0
        ),
        compiler_params=pltpu.CompilerParams(vmem_limit_bytes=1024 * 1024),
        name="load",
    )(*[pltpu.with_memory_space_constraint(a, pltpu.HBM) for a, _, _ in parts])


def add_kernel(own_ref, other_ref, *refs):
    pieces, outs = [refs[k][...] for k in (0, 3, 1, 2)], refs[4:]
    rows = outs[0].shape[0]
    width = pieces[0].shape[1]
    device = lax.axis_index("pool")
    columns = pl.ds(pl.multiple_of(device // 4 * (4 * width), 4 * width), 4 * width)
    base = []
    for place in range(4):
        piece = pieces[0]
        for mask in (1, 2, 3):
            piece = jnp.where(device % 4 == place ^ mask, pieces[mask], piece)
        base.append(piece)
    base = jnp.concatenate(base, axis=1)
    both = own_ref[...].astype(jnp.float32) + other_ref[...].astype(jnp.float32)
    part = own_ref[:, columns].astype(jnp.float32) + other_ref[:, columns].astype(jnp.float32) + base
    for k, out in enumerate(outs):
        span = slice(k * rows, (k + 1) * rows)
        out[...] = both[span].astype(jnp.bfloat16)
        out[:, columns] = part[span].astype(jnp.bfloat16)


def sum_kernel(*refs):
    total = refs[0][...].astype(jnp.float32)
    for ref in refs[1:-1]:
        total += ref[...].astype(jnp.float32)
    refs[-1][...] = total.astype(jnp.bfloat16)


def body(
    tokens,
    base_projection_weight,
    adapter_down_weight,
    adapter_up_weight,
    request_adapter,
    adapter_block_count,
    adapter_store_slot,
):
    devices = lax.axis_size("pool")
    rows, model = tokens.shape
    half = devices // 2 * rows
    vmem, smem = pl.BlockSpec(memory_space=pltpu.VMEM), pl.BlockSpec(memory_space=pltpu.SMEM)
    params = pltpu.CompilerParams(vmem_limit_bytes=8 * 1024 * 1024)

    down2 = exchange(adapter_down_weight, 1, devices)
    up2 = exchange(adapter_up_weight, 1, devices)
    extent = adapter_down_weight.shape[0]
    mask = pl.pallas_call(
        functools.partial(mask_kernel, rows, extent),
        out_shape=jax.ShapeDtypeStruct((half, 2 * extent), jnp.float32),
        in_specs=[smem] * 3,
        out_specs=vmem,
        compiler_params=params,
        name="mask",
    )(request_adapter[:, 0], adapter_block_count, adapter_store_slot)
    weight, down, up = base_projection_weight, adapter_down_weight, adapter_up_weight
    cut = model // 2
    near, head = load((tokens, 0, rows), (weight, 0, cut))
    for k, stage in enumerate(stages_of(devices)):
        got = [exchange(near if k else tokens, m, devices) for m in stage]
        if k == 0:
            near, head, got = lax.optimization_barrier((near, head, got))
        if k == 1:
            weight, down, up, near = lax.optimization_barrier((weight, down, up, near))
            (tail,) = load((weight, cut, model))
            near, tail, mask, *got = lax.optimization_barrier((near, tail, mask, *got[::-1]))
            got = got[::-1]
        near = jnp.concatenate([near] + got, axis=0)
    far = exchange(near, 1, devices)

    shrink = pl.pallas_call(
        functools.partial(shrink_kernel, rows),
        out_shape=jax.ShapeDtypeStruct((half, 2 * extent), jnp.bfloat16),
        in_specs=[vmem] * 4,
        out_specs=vmem,
        compiler_params=params,
        name="shrink",
    )(mask, near, down, down2)
    own, other = pl.pallas_call(
        delta_kernel,
        out_shape=[jax.ShapeDtypeStruct((half // 2, model), jnp.bfloat16)] * 2,
        in_specs=[vmem] * 3,
        out_specs=[vmem] * 2,
        compiler_params=params,
        name="delta",
    )(shrink, up, up2)
    other = exchange(other, 2, devices)
    far, own = lax.optimization_barrier((far, own))
    base = pl.pallas_call(
        functools.partial(base_kernel, rows),
        out_shape=[jax.ShapeDtypeStruct((half // 2, weight.shape[1]), jnp.float32)] * 4,
        in_specs=[vmem] * 4,
        out_specs=[vmem] * 4,
        compiler_params=params,
        name="base",
    )(near, far, head, tail)
    base = [base[0], exchange(base[2], 1, devices), exchange(base[1], 2, devices), exchange(base[3], 3, devices)]
    sums = pl.pallas_call(
        add_kernel,
        out_shape=[jax.ShapeDtypeStruct((rows, model), jnp.bfloat16)] * (devices // 4),
        in_specs=[vmem] * 6,
        out_specs=[vmem] * (devices // 4),
        compiler_params=params,
        name="add",
    )(own, other, base[0], base[2], base[3], base[1])
    got = [exchange(sums[k], 4 * k, devices) for k in range(1, devices // 4)]
    return pl.pallas_call(
        sum_kernel,
        out_shape=jax.ShapeDtypeStruct((rows, model), jnp.bfloat16),
        in_specs=[vmem] * (devices // 4),
        out_specs=vmem,
        compiler_params=params,
        name="sum",
    )(sums[0], *got[::-1])


def solution(mesh):
    return jax.shard_map(
        body,
        mesh=mesh,
        in_specs=(
            P(("groups", "pool"), None),
            P(None, "pool"),
            P("pool", None),
            P("pool", None),
            P("groups", None),
            P(),
            P(),
        ),
        out_specs=P(("groups", "pool"), None),
        check_vma=False,
    )
```

```python
import functools

import jax
import jax.numpy as jnp
from jax import lax
from jax.experimental import pallas as pl
from jax.experimental.pallas import tpu as pltpu
from jax.sharding import PartitionSpec as P

RANK_BLOCK = 16
LANES = 128


def stages_of(devices):
    bits = [1 << k for k in range(1, devices.bit_length() - 1)]
    stages = [[b] for b in bits[:1]]
    rest = bits[1:]
    for k in range(0, len(rest), 2):
        low = rest[k]
        stages.append([low, rest[k + 1], low + rest[k + 1]] if k + 1 < len(rest) else [low])
    return stages


def exchange(array, mask, devices):
    return lax.ppermute(array, "pool", [(d, d ^ mask) for d in range(devices)])


def by_y(rows, array):
    blocks = [array[r : r + rows] for r in range(0, array.shape[0], rows)]
    return jnp.concatenate(blocks[::2] + blocks[1::2], axis=0)


def mask_kernel(rows, extent, ident_ref, count_ref, slot_ref, out_ref):
    half = out_ref.shape[0]
    requests, adapters = ident_ref.shape[1], slot_ref.shape[1]
    device = lax.axis_index("pool")
    slots, counts = slot_ref[...], count_ref[...]
    rank = jnp.sum(jnp.where(slots == device, counts, 0), axis=1, keepdims=True) * RANK_BLOCK
    rank2 = jnp.sum(jnp.where(slots == device ^ 1, counts, 0), axis=1, keepdims=True) * RANK_BLOCK
    row = lax.broadcasted_iota(jnp.int32, (half, requests), 0)
    chip = row % (half // 2) // rows * 2 + row // (half // 2)
    request = (device ^ (2 * chip)) * rows + row % rows
    picked = request == lax.broadcasted_iota(jnp.int32, (half, requests), 1)
    ident = jnp.sum(jnp.where(picked, ident_ref[...], 0), axis=1, keepdims=True)
    named = ident == lax.broadcasted_iota(jnp.int32, (half, adapters), 1)
    slot = jnp.sum(jnp.where(named, slots, 0), axis=1, keepdims=True)
    col = lax.broadcasted_iota(jnp.int32, (half, extent), 1)
    out_ref[:, :extent] = jnp.where((slot == device) & (col < rank), 1.0, 0.0)
    out_ref[:, extent:] = jnp.where((slot == device ^ 1) & (col < rank2), 1.0, 0.0)


def shrink_kernel(rows, mask_ref, near_ref, down_ref, down2_ref, out_ref):
    near = near_ref[...]
    shrink = jnp.concatenate(
        [
            lax.dot_general(near, ref[...], (((1,), (1,)), ((), ())), preferred_element_type=jnp.float32)
            for ref in (down_ref, down2_ref)
        ],
        axis=1,
    )
    out_ref[...] = jnp.where(mask_ref[...] > 0, by_y(rows, shrink), 0.0).astype(jnp.bfloat16)


def delta_kernel(shrink_ref, up_ref, up2_ref, own_out, other_out):
    extent, model = up_ref.shape
    part = own_out.shape[0]
    step = min(1024, model)
    for c in range(0, model, step):
        span = slice(c, c + step)
        delta = jnp.dot(
            shrink_ref[:, :extent], up_ref[:, span], preferred_element_type=jnp.float32
        ) + jnp.dot(shrink_ref[:, extent:], up2_ref[:, span], preferred_element_type=jnp.float32)
        own_out[:, span] = delta[:part].astype(jnp.bfloat16)
        other_out[:, span] = delta[part:].astype(jnp.bfloat16)


def base_kernel(rows, near_ref, far_ref, weight_ref, weight2_ref, *outs):
    part = outs[0].shape[0]
    cut = weight_ref.shape[0]
    x = jnp.concatenate([near_ref[...], far_ref[...]], axis=0)
    base = jnp.dot(x[:, :cut], weight_ref[...], preferred_element_type=jnp.float32)
    base += jnp.dot(x[:, cut:], weight2_ref[...], preferred_element_type=jnp.float32)
    for k in (0, 2):
        placed = by_y(rows, base[k * part : (k + 2) * part])
        outs[k][...] = placed[:part]
        outs[k + 1][...] = placed[part:]


def load_kernel(starts, *refs):
    count = len(starts)
    copies = []
    for i, start in enumerate(starts):
        held = refs[count + i]
        source = refs[i].at[pl.ds(start, held.shape[0])]
        copies.append(pltpu.make_async_copy(source, held, refs[2 * count].at[i]))
    for copy in copies:
        copy.start()
    for copy in copies:
        copy.wait()


def load(*parts):
    count = len(parts)
    shapes = [((stop - start, a.shape[1]), a.dtype) for a, start, stop in parts]
    return pl.pallas_call(
        functools.partial(load_kernel, [start for _, start, _ in parts]),
        out_shape=[pltpu.VMEM(*shape) for shape in shapes],
        in_specs=[pl.BlockSpec(memory_space=pltpu.HBM)] * count,
        out_specs=[pl.BlockSpec(memory_space=pltpu.VMEM)] * count,
        scratch_shapes=[pltpu.SemaphoreType.DMA((count,))],
        cost_estimate=pl.CostEstimate(
            flops=0, bytes_accessed=sum(4 * dims[0] * dims[1] for dims, _ in shapes), transcendentals=0
        ),
        compiler_params=pltpu.CompilerParams(vmem_limit_bytes=1024 * 1024),
        name="load",
    )(*[pltpu.with_memory_space_constraint(a, pltpu.HBM) for a, _, _ in parts])


def add_kernel(own_ref, other_ref, *refs):
    pieces, outs = [refs[k][...] for k in (0, 3, 1, 2)], refs[4:]
    rows = outs[0].shape[0]
    width = pieces[0].shape[1]
    device = lax.axis_index("pool")
    columns = pl.ds(pl.multiple_of(device // 4 * (4 * width), 4 * width), 4 * width)
    base = []
    for place in range(4):
        piece = pieces[0]
        for mask in (1, 2, 3):
            piece = jnp.where(device % 4 == place ^ mask, pieces[mask], piece)
        base.append(piece)
    base = jnp.concatenate(base, axis=1)
    both = own_ref[...].astype(jnp.float32) + other_ref[...].astype(jnp.float32)
    part = own_ref[:, columns].astype(jnp.float32) + other_ref[:, columns].astype(jnp.float32) + base
    for k, out in enumerate(outs):
        span = slice(k * rows, (k + 1) * rows)
        out[...] = both[span].astype(jnp.bfloat16)
        out[:, columns] = part[span].astype(jnp.bfloat16)


def sum_kernel(*refs):
    total = refs[0][...].astype(jnp.float32)
    for ref in refs[1:-1]:
        total += ref[...].astype(jnp.float32)
    refs[-1][...] = total.astype(jnp.bfloat16)


def body(
    tokens,
    base_projection_weight,
    adapter_down_weight,
    adapter_up_weight,
    request_adapter,
    adapter_block_count,
    adapter_store_slot,
):
    devices = lax.axis_size("pool")
    rows, model = tokens.shape
    half = devices // 2 * rows
    vmem = pl.BlockSpec(memory_space=pltpu.VMEM)
    params = pltpu.CompilerParams(vmem_limit_bytes=8 * 1024 * 1024)

    down2 = exchange(adapter_down_weight, 1, devices)
    up2 = exchange(adapter_up_weight, 1, devices)
    extent = adapter_down_weight.shape[0]
    mask = pl.pallas_call(
        functools.partial(mask_kernel, rows, extent),
        out_shape=jax.ShapeDtypeStruct((half, 2 * extent), jnp.float32),
        in_specs=[vmem] * 3,
        out_specs=vmem,
        compiler_params=params,
        name="mask",
    )(request_adapter.reshape(1, -1), adapter_block_count[None], adapter_store_slot[None])
    weight, down, up = base_projection_weight, adapter_down_weight, adapter_up_weight
    cut = model // 4
    near, head, up = load((tokens, 0, rows), (weight, 0, cut), (up, 0, extent))
    for k, stage in enumerate(stages_of(devices)):
        got = [exchange(near if k else tokens, m, devices) for m in stage]
        if k == 0:
            near, head, up, got = lax.optimization_barrier((near, head, up, got))
        if k == 1:
            weight, down, up, near = lax.optimization_barrier((weight, down, up, near))
            (tail,) = load((weight, cut, model))
            near, tail, mask, *got = lax.optimization_barrier((near, tail, mask, *got[::-1]))
            got = got[::-1]
        near = jnp.concatenate([near] + got, axis=0)
    far = exchange(near, 1, devices)

    shrink = pl.pallas_call(
        functools.partial(shrink_kernel, rows),
        out_shape=jax.ShapeDtypeStruct((half, 2 * extent), jnp.bfloat16),
        in_specs=[vmem] * 4,
        out_specs=vmem,
        compiler_params=params,
        name="shrink",
    )(mask, near, down, down2)
    own, other = pl.pallas_call(
        delta_kernel,
        out_shape=[jax.ShapeDtypeStruct((half // 2, model), jnp.bfloat16)] * 2,
        in_specs=[vmem] * 3,
        out_specs=[vmem] * 2,
        compiler_params=params,
        name="delta",
    )(shrink, up, up2)
    other = exchange(other, 2, devices)
    far, own = lax.optimization_barrier((far, own))
    base = pl.pallas_call(
        functools.partial(base_kernel, rows),
        out_shape=[jax.ShapeDtypeStruct((half // 2, weight.shape[1]), jnp.float32)] * 4,
        in_specs=[vmem] * 4,
        out_specs=[vmem] * 4,
        compiler_params=params,
        name="base",
    )(near, far, head, tail)
    base = [base[0], exchange(base[2], 1, devices), exchange(base[1], 2, devices), exchange(base[3], 3, devices)]
    sums = pl.pallas_call(
        add_kernel,
        out_shape=[jax.ShapeDtypeStruct((rows, model), jnp.bfloat16)] * (devices // 4),
        in_specs=[vmem] * 6,
        out_specs=[vmem] * (devices // 4),
        compiler_params=params,
        name="add",
    )(own, other, base[0], base[2], base[3], base[1])
    got = [exchange(sums[k], 4 * k, devices) for k in range(1, devices // 4)]
    return pl.pallas_call(
        sum_kernel,
        out_shape=jax.ShapeDtypeStruct((rows, model), jnp.bfloat16),
        in_specs=[vmem] * (devices // 4),
        out_specs=vmem,
        compiler_params=params,
        name="sum",
    )(sums[0], *got[::-1])


def solution(mesh):
    return jax.shard_map(
        body,
        mesh=mesh,
        in_specs=(
            P(("groups", "pool"), None),
            P(None, "pool"),
            P("pool", None),
            P("pool", None),
            P("groups", None),
            P(),
            P(),
        ),
        out_specs=P(("groups", "pool"), None),
        check_vma=False,
    )
```

```python
import functools

import jax
import jax.numpy as jnp
from jax import lax
from jax.experimental import pallas as pl
from jax.experimental.pallas import tpu as pltpu
from jax.sharding import PartitionSpec as P

RANK_BLOCK = 16
LANES = 128


def stages_of(devices):
    bits = [1 << k for k in range(1, devices.bit_length() - 1)]
    stages = [[b] for b in bits[-1:]]
    rest = bits[:-1]
    for k in range(0, len(rest), 2):
        low = rest[k]
        stages.append([low, rest[k + 1], low + rest[k + 1]] if k + 1 < len(rest) else [low])
    return stages


def order_of(devices):
    held = [0]
    for stage in stages_of(devices):
        held += [mask ^ h for mask in stage for h in held]
    return held


def exchange(array, mask, devices):
    return lax.ppermute(array, "pool", [(d, d ^ mask) for d in range(devices)])


def by_y(rows, array):
    held = order_of(2 * array.shape[0] // rows)
    places = sorted(range(len(held)), key=lambda k: (held[k] & 2, held[k]))
    return jnp.concatenate([array[k * rows : (k + 1) * rows] for k in places], axis=0)


def mask_kernel(rows, extent, ident_ref, count_ref, slot_ref, out_ref):
    half = out_ref.shape[0]
    requests, adapters = ident_ref.shape[1], slot_ref.shape[1]
    device = lax.axis_index("pool")
    slots, counts = slot_ref[...], count_ref[...]
    rank = jnp.sum(jnp.where(slots == device, counts, 0), axis=1, keepdims=True) * RANK_BLOCK
    rank2 = jnp.sum(jnp.where(slots == device ^ 1, counts, 0), axis=1, keepdims=True) * RANK_BLOCK
    row = lax.broadcasted_iota(jnp.int32, (half, requests), 0)
    chip = row % (half // 2) // rows * 2 + row // (half // 2)
    request = (device ^ (2 * chip)) * rows + row % rows
    picked = request == lax.broadcasted_iota(jnp.int32, (half, requests), 1)
    ident = jnp.sum(jnp.where(picked, ident_ref[...], 0), axis=1, keepdims=True)
    named = ident == lax.broadcasted_iota(jnp.int32, (half, adapters), 1)
    slot = jnp.sum(jnp.where(named, slots, 0), axis=1, keepdims=True)
    col = lax.broadcasted_iota(jnp.int32, (half, extent), 1)
    out_ref[:, :extent] = jnp.where((slot == device) & (col < rank), 1.0, 0.0)
    out_ref[:, extent:] = jnp.where((slot == device ^ 1) & (col < rank2), 1.0, 0.0)


def shrink_kernel(rows, mask_ref, near_ref, down_ref, down2_ref, out_ref):
    near = near_ref[...]
    shrink = jnp.concatenate(
        [
            lax.dot_general(near, ref[...], (((1,), (1,)), ((), ())), preferred_element_type=jnp.float32)
            for ref in (down_ref, down2_ref)
        ],
        axis=1,
    )
    out_ref[...] = jnp.where(mask_ref[...] > 0, by_y(rows, shrink), 0.0).astype(jnp.bfloat16)


def delta_kernel(shrink_ref, up_ref, up2_ref, own_out, other_out):
    extent, model = up_ref.shape
    part = own_out.shape[0]
    step = min(1024, model)
    for c in range(0, model, step):
        span = slice(c, c + step)
        delta = jnp.dot(
            shrink_ref[:, :extent], up_ref[:, span], preferred_element_type=jnp.float32
        ) + jnp.dot(shrink_ref[:, extent:], up2_ref[:, span], preferred_element_type=jnp.float32)
        own_out[:, span] = delta[:part].astype(jnp.bfloat16)
        other_out[:, span] = delta[part:].astype(jnp.bfloat16)


def base_kernel(rows, near_ref, far_ref, weight_ref, weight2_ref, *outs):
    part = outs[0].shape[0]
    cut = weight_ref.shape[0]
    x = jnp.concatenate([near_ref[...], far_ref[...]], axis=0)
    base = jnp.dot(x[:, :cut], weight_ref[...], preferred_element_type=jnp.float32)
    base += jnp.dot(x[:, cut:], weight2_ref[...], preferred_element_type=jnp.float32)
    for k in (0, 2):
        placed = by_y(rows, base[k * part : (k + 2) * part])
        outs[k][...] = placed[:part]
        outs[k + 1][...] = placed[part:]


def load_kernel(starts, *refs):
    count = len(starts)
    copies = []
    for i, start in enumerate(starts):
        held = refs[count + i]
        source = refs[i].at[pl.ds(start, held.shape[0])]
        copies.append(pltpu.make_async_copy(source, held, refs[2 * count].at[i]))
    for copy in copies:
        copy.start()
    for copy in copies:
        copy.wait()


def load(*parts):
    count = len(parts)
    shapes = [((stop - start, a.shape[1]), a.dtype) for a, start, stop in parts]
    return pl.pallas_call(
        functools.partial(load_kernel, [start for _, start, _ in parts]),
        out_shape=[pltpu.VMEM(*shape) for shape in shapes],
        in_specs=[pl.BlockSpec(memory_space=pltpu.HBM)] * count,
        out_specs=[pl.BlockSpec(memory_space=pltpu.VMEM)] * count,
        scratch_shapes=[pltpu.SemaphoreType.DMA((count,))],
        cost_estimate=pl.CostEstimate(
            flops=0, bytes_accessed=sum(4 * dims[0] * dims[1] for dims, _ in shapes), transcendentals=0
        ),
        compiler_params=pltpu.CompilerParams(vmem_limit_bytes=1024 * 1024),
        name="load",
    )(*[pltpu.with_memory_space_constraint(a, pltpu.HBM) for a, _, _ in parts])


def add_kernel(own_ref, other_ref, *refs):
    pieces, outs = [refs[k][...] for k in (0, 3, 1, 2)], refs[4:]
    rows = outs[0].shape[0]
    width = pieces[0].shape[1]
    device = lax.axis_index("pool")
    columns = pl.ds(pl.multiple_of(device // 4 * (4 * width), 4 * width), 4 * width)
    base = []
    for place in range(4):
        piece = pieces[0]
        for mask in (1, 2, 3):
            piece = jnp.where(device % 4 == place ^ mask, pieces[mask], piece)
        base.append(piece)
    base = jnp.concatenate(base, axis=1)
    both = own_ref[...].astype(jnp.float32) + other_ref[...].astype(jnp.float32)
    part = own_ref[:, columns].astype(jnp.float32) + other_ref[:, columns].astype(jnp.float32) + base
    for k, out in enumerate(outs):
        span = slice(k * rows, (k + 1) * rows)
        out[...] = both[span].astype(jnp.bfloat16)
        out[:, columns] = part[span].astype(jnp.bfloat16)


def sum_kernel(*refs):
    total = refs[0][...].astype(jnp.float32)
    for ref in refs[1:-1]:
        total += ref[...].astype(jnp.float32)
    refs[-1][...] = total.astype(jnp.bfloat16)


def body(
    tokens,
    base_projection_weight,
    adapter_down_weight,
    adapter_up_weight,
    request_adapter,
    adapter_block_count,
    adapter_store_slot,
):
    devices = lax.axis_size("pool")
    rows, model = tokens.shape
    half = devices // 2 * rows
    vmem = pl.BlockSpec(memory_space=pltpu.VMEM)
    params = pltpu.CompilerParams(vmem_limit_bytes=8 * 1024 * 1024)

    down2 = exchange(adapter_down_weight, 1, devices)
    up2 = exchange(adapter_up_weight, 1, devices)
    extent = adapter_down_weight.shape[0]
    mask = pl.pallas_call(
        functools.partial(mask_kernel, rows, extent),
        out_shape=jax.ShapeDtypeStruct((half, 2 * extent), jnp.float32),
        in_specs=[vmem] * 3,
        out_specs=vmem,
        compiler_params=params,
        name="mask",
    )(request_adapter.reshape(1, -1), adapter_block_count[None], adapter_store_slot[None])
    weight, down, up = base_projection_weight, adapter_down_weight, adapter_up_weight
    cut = model * 5 // 8
    near, head, up = load((tokens, 0, rows), (weight, 0, cut), (up, 0, extent))
    for k, stage in enumerate(stages_of(devices)):
        got = [exchange(near if k else tokens, m, devices) for m in stage]
        if k == 0:
            near, head, up, got = lax.optimization_barrier((near, head, up, got))
        if k == 1:
            weight, down, up, near = lax.optimization_barrier((weight, down, up, near))
            (tail,) = load((weight, cut, model))
            near, tail, mask, *got = lax.optimization_barrier((near, tail, mask, *[got[i] for i in (2, 0, 1)]))
            got = [got[i] for i in [1, 2, 0]]
        near = jnp.concatenate([near] + got, axis=0)
    far = exchange(near, 1, devices)

    shrink = pl.pallas_call(
        functools.partial(shrink_kernel, rows),
        out_shape=jax.ShapeDtypeStruct((half, 2 * extent), jnp.bfloat16),
        in_specs=[vmem] * 4,
        out_specs=vmem,
        compiler_params=params,
        name="shrink",
    )(mask, near, down, down2)
    own, other = pl.pallas_call(
        delta_kernel,
        out_shape=[jax.ShapeDtypeStruct((half // 2, model), jnp.bfloat16)] * 2,
        in_specs=[vmem] * 3,
        out_specs=[vmem] * 2,
        compiler_params=params,
        name="delta",
    )(shrink, up, up2)
    other = exchange(other, 2, devices)
    far, own = lax.optimization_barrier((far, own))
    base = pl.pallas_call(
        functools.partial(base_kernel, rows),
        out_shape=[jax.ShapeDtypeStruct((half // 2, weight.shape[1]), jnp.float32)] * 4,
        in_specs=[vmem] * 4,
        out_specs=[vmem] * 4,
        compiler_params=params,
        name="base",
    )(near, far, head, tail)
    base = [base[0], exchange(base[2], 1, devices), exchange(base[1], 2, devices), exchange(base[3], 3, devices)]
    sums = pl.pallas_call(
        add_kernel,
        out_shape=[jax.ShapeDtypeStruct((rows, model), jnp.bfloat16)] * (devices // 4),
        in_specs=[vmem] * 6,
        out_specs=[vmem] * (devices // 4),
        compiler_params=params,
        name="add",
    )(own, other, base[0], base[2], base[3], base[1])
    got = [exchange(sums[k], 4 * k, devices) for k in range(1, devices // 4)]
    return pl.pallas_call(
        sum_kernel,
        out_shape=jax.ShapeDtypeStruct((rows, model), jnp.bfloat16),
        in_specs=[vmem] * (devices // 4),
        out_specs=vmem,
        compiler_params=params,
        name="sum",
    )(sums[0], *got[::-1])


def solution(mesh):
    return jax.shard_map(
        body,
        mesh=mesh,
        in_specs=(
            P(("groups", "pool"), None),
            P(None, "pool"),
            P("pool", None),
            P("pool", None),
            P("groups", None),
            P(),
            P(),
        ),
        out_specs=P(("groups", "pool"), None),
        check_vma=False,
    )
```

```python
import functools

import jax
import jax.numpy as jnp
from jax import lax
from jax.experimental import pallas as pl
from jax.experimental.pallas import tpu as pltpu
from jax.sharding import PartitionSpec as P

RANK_BLOCK = 16
LANES = 128


def stages_of(devices):
    bits = [1 << k for k in range(1, devices.bit_length() - 1)]
    stages = [[b] for b in bits[-1:]]
    rest = bits[:-1]
    for k in range(0, len(rest), 2):
        low = rest[k]
        stages.append([low, rest[k + 1], low + rest[k + 1]] if k + 1 < len(rest) else [low])
    return stages


def order_of(devices):
    held = [0]
    for stage in stages_of(devices):
        held += [mask ^ h for mask in stage for h in held]
    return held


def exchange(array, mask, devices):
    return lax.ppermute(array, "pool", [(d, d ^ mask) for d in range(devices)])


def by_y(rows, array):
    held = order_of(2 * array.shape[0] // rows)
    places = sorted(range(len(held)), key=lambda k: (held[k] & 2, held[k]))
    return jnp.concatenate([array[k * rows : (k + 1) * rows] for k in places], axis=0)


def mask_kernel(rows, extent, ident_ref, count_ref, slot_ref, out_ref):
    half = out_ref.shape[0]
    requests, adapters = ident_ref.shape[1], slot_ref.shape[1]
    device = lax.axis_index("pool")
    slots, counts = slot_ref[...], count_ref[...]
    rank = jnp.sum(jnp.where(slots == device, counts, 0), axis=1, keepdims=True) * RANK_BLOCK
    rank2 = jnp.sum(jnp.where(slots == device ^ 1, counts, 0), axis=1, keepdims=True) * RANK_BLOCK
    row = lax.broadcasted_iota(jnp.int32, (half, requests), 0)
    chip = row % (half // 2) // rows * 2 + row // (half // 2)
    request = (device ^ (2 * chip)) * rows + row % rows
    picked = request == lax.broadcasted_iota(jnp.int32, (half, requests), 1)
    ident = jnp.sum(jnp.where(picked, ident_ref[...], 0), axis=1, keepdims=True)
    named = ident == lax.broadcasted_iota(jnp.int32, (half, adapters), 1)
    slot = jnp.sum(jnp.where(named, slots, 0), axis=1, keepdims=True)
    col = lax.broadcasted_iota(jnp.int32, (half, extent), 1)
    out_ref[:, :extent] = jnp.where((slot == device) & (col < rank), 1.0, 0.0)
    out_ref[:, extent:] = jnp.where((slot == device ^ 1) & (col < rank2), 1.0, 0.0)


def shrink_kernel(rows, mask_ref, near_ref, down_ref, down2_ref, out_ref):
    near = near_ref[...]
    shrink = jnp.concatenate(
        [
            lax.dot_general(near, ref[...], (((1,), (1,)), ((), ())), preferred_element_type=jnp.float32)
            for ref in (down_ref, down2_ref)
        ],
        axis=1,
    )
    out_ref[...] = jnp.where(mask_ref[...] > 0, by_y(rows, shrink), 0.0).astype(jnp.bfloat16)


def delta_kernel(shrink_ref, up_ref, up2_ref, own_out, other_out):
    extent, model = up_ref.shape
    part = own_out.shape[0]
    step = min(1024, model)
    for c in range(0, model, step):
        span = slice(c, c + step)
        delta = jnp.dot(
            shrink_ref[:, :extent], up_ref[:, span], preferred_element_type=jnp.float32
        ) + jnp.dot(shrink_ref[:, extent:], up2_ref[:, span], preferred_element_type=jnp.float32)
        own_out[:, span] = delta[:part].astype(jnp.bfloat16)
        other_out[:, span] = delta[part:].astype(jnp.bfloat16)


def base_kernel(rows, near_ref, far_ref, weight_ref, weight2_ref, *outs):
    part = outs[0].shape[0]
    cut = weight_ref.shape[0]
    x = jnp.concatenate([near_ref[...], far_ref[...]], axis=0)
    base = jnp.dot(x[:, :cut], weight_ref[...], preferred_element_type=jnp.float32)
    base += jnp.dot(x[:, cut:], weight2_ref[...], preferred_element_type=jnp.float32)
    for k in (0, 2):
        placed = by_y(rows, base[k * part : (k + 2) * part])
        outs[k][...] = placed[:part]
        outs[k + 1][...] = placed[part:]


def load_kernel(starts, *refs):
    count = len(starts)
    copies = []
    for i, start in enumerate(starts):
        held = refs[count + i]
        source = refs[i].at[pl.ds(start, held.shape[0])]
        copies.append(pltpu.make_async_copy(source, held, refs[2 * count].at[i]))
    for copy in copies:
        copy.start()
    for copy in copies:
        copy.wait()


def load(*parts):
    count = len(parts)
    shapes = [((stop - start, a.shape[1]), a.dtype) for a, start, stop in parts]
    return pl.pallas_call(
        functools.partial(load_kernel, [start for _, start, _ in parts]),
        out_shape=[pltpu.VMEM(*shape) for shape in shapes],
        in_specs=[pl.BlockSpec(memory_space=pltpu.HBM)] * count,
        out_specs=[pl.BlockSpec(memory_space=pltpu.VMEM)] * count,
        scratch_shapes=[pltpu.SemaphoreType.DMA((count,))],
        cost_estimate=pl.CostEstimate(
            flops=0, bytes_accessed=sum(4 * dims[0] * dims[1] for dims, _ in shapes), transcendentals=0
        ),
        compiler_params=pltpu.CompilerParams(vmem_limit_bytes=1024 * 1024),
        name="load",
    )(*[pltpu.with_memory_space_constraint(a, pltpu.HBM) for a, _, _ in parts])


def add_kernel(own_ref, other_ref, *refs):
    pieces, outs = [refs[k][...] for k in (0, 3, 1, 2)], refs[4:]
    rows = outs[0].shape[0]
    width = pieces[0].shape[1]
    device = lax.axis_index("pool")
    columns = pl.ds(pl.multiple_of(device // 4 * (4 * width), 4 * width), 4 * width)
    base = []
    for place in range(4):
        piece = pieces[0]
        for mask in (1, 2, 3):
            piece = jnp.where(device % 4 == place ^ mask, pieces[mask], piece)
        base.append(piece)
    base = jnp.concatenate(base, axis=1)
    both = own_ref[...].astype(jnp.float32) + other_ref[...].astype(jnp.float32)
    part = own_ref[:, columns].astype(jnp.float32) + other_ref[:, columns].astype(jnp.float32) + base
    for k, out in enumerate(outs):
        span = slice(k * rows, (k + 1) * rows)
        out[...] = both[span].astype(jnp.bfloat16)
        out[:, columns] = part[span].astype(jnp.bfloat16)


def sum_kernel(*refs):
    total = refs[0][...].astype(jnp.float32)
    for ref in refs[1:-1]:
        total += ref[...].astype(jnp.float32)
    refs[-1][...] = total.astype(jnp.bfloat16)


def body(
    tokens,
    base_projection_weight,
    adapter_down_weight,
    adapter_up_weight,
    request_adapter,
    adapter_block_count,
    adapter_store_slot,
):
    devices = lax.axis_size("pool")
    rows, model = tokens.shape
    half = devices // 2 * rows
    vmem = pl.BlockSpec(memory_space=pltpu.VMEM)
    params = pltpu.CompilerParams(vmem_limit_bytes=8 * 1024 * 1024)

    down2 = exchange(adapter_down_weight, 1, devices)
    up2 = exchange(adapter_up_weight, 1, devices)
    extent = adapter_down_weight.shape[0]
    mask = pl.pallas_call(
        functools.partial(mask_kernel, rows, extent),
        out_shape=jax.ShapeDtypeStruct((half, 2 * extent), jnp.float32),
        in_specs=[vmem] * 3,
        out_specs=vmem,
        compiler_params=params,
        name="mask",
    )(request_adapter.reshape(1, -1), adapter_block_count[None], adapter_store_slot[None])
    weight, down, up = base_projection_weight, adapter_down_weight, adapter_up_weight
    cut = model * 11 // 16
    near, head, up = load((tokens, 0, rows), (weight, 0, cut), (up, 0, extent))
    for k, stage in enumerate(stages_of(devices)):
        got = [exchange(near if k else tokens, m, devices) for m in stage]
        if k == 0:
            near, head, up, got = lax.optimization_barrier((near, head, up, got))
        if k == 1:
            weight, down, up, near = lax.optimization_barrier((weight, down, up, near))
            (tail,) = load((weight, cut, model))
            near, tail, mask, *got = lax.optimization_barrier((near, tail, mask, *[got[i] for i in (2, 0, 1)]))
            got = [got[i] for i in [1, 2, 0]]
        near = jnp.concatenate([near] + got, axis=0)
    far = exchange(near, 1, devices)

    shrink = pl.pallas_call(
        functools.partial(shrink_kernel, rows),
        out_shape=jax.ShapeDtypeStruct((half, 2 * extent), jnp.bfloat16),
        in_specs=[vmem] * 4,
        out_specs=vmem,
        compiler_params=params,
        name="shrink",
    )(mask, near, down, down2)
    own, other = pl.pallas_call(
        delta_kernel,
        out_shape=[jax.ShapeDtypeStruct((half // 2, model), jnp.bfloat16)] * 2,
        in_specs=[vmem] * 3,
        out_specs=[vmem] * 2,
        compiler_params=params,
        name="delta",
    )(shrink, up, up2)
    other = exchange(other, 2, devices)
    far, own = lax.optimization_barrier((far, own))
    base = pl.pallas_call(
        functools.partial(base_kernel, rows),
        out_shape=[jax.ShapeDtypeStruct((half // 2, weight.shape[1]), jnp.float32)] * 4,
        in_specs=[vmem] * 4,
        out_specs=[vmem] * 4,
        compiler_params=params,
        name="base",
    )(near, far, head, tail)
    base = [base[0], exchange(base[2], 1, devices), exchange(base[1], 2, devices), exchange(base[3], 3, devices)]
    sums = pl.pallas_call(
        add_kernel,
        out_shape=[jax.ShapeDtypeStruct((rows, model), jnp.bfloat16)] * (devices // 4),
        in_specs=[vmem] * 6,
        out_specs=[vmem] * (devices // 4),
        compiler_params=params,
        name="add",
    )(own, other, base[0], base[2], base[3], base[1])
    got = [exchange(sums[k], 4 * k, devices) for k in range(1, devices // 4)]
    return pl.pallas_call(
        sum_kernel,
        out_shape=jax.ShapeDtypeStruct((rows, model), jnp.bfloat16),
        in_specs=[vmem] * (devices // 4),
        out_specs=vmem,
        compiler_params=params,
        name="sum",
    )(sums[0], *got[::-1])


def solution(mesh):
    return jax.shard_map(
        body,
        mesh=mesh,
        in_specs=(
            P(("groups", "pool"), None),
            P(None, "pool"),
            P("pool", None),
            P("pool", None),
            P("groups", None),
            P(),
            P(),
        ),
        out_specs=P(("groups", "pool"), None),
        check_vma=False,
    )
```
